256 devices in a mesh: item: 8 (over z), user: 16 (over x, y), tp: 2 (over core).
Axes of the slice: x: 4, y: 4, z: 8, core: 2. Of those that a mesh axis runs over, the one named last changes fastest.
Arguments:
- item_states: bfloat16 [2048, 4096], P('item', ('user', 'tp')), may hold values from -6 to 6
- w_gate: bfloat16 [4096, 8448], P(None, ('user', 'tp')), may hold values from -0.09375 to 0.09375
- w_up: bfloat16 [4096, 8448], P(None, ('user', 'tp')), may hold values from -0.09375 to 0.09375
- w_down: bfloat16 [8448, 4096], P(('user', 'tp')), may hold values from -0.0625 to 0.0625
- w_qkv: bfloat16 [4096, 3, 2048], P(None, None, ('item', 'tp')), may hold values from -0.09375 to 0.09375
- w_out: bfloat16 [2048, 4096], P(('item', 'tp')), may hold values from -0.125 to 0.125
- hist_ids: int32 [16, 256], P('user'), may hold values from 0 to 2047
- hist_lengths: int32 [16, 16], P('user'), may hold values from 1 to 64, 256 in all within a row
- neg_ids: int32 [16, 384], P('user'), may hold values from 0 to 2047
Outputs:
- loss: float32 [16], P('user')
- user_out: bfloat16 [16, 256, 4096], P('user')
- item_grad: float32 [2048, 4096], P(('item', 'user'), 'tp')
The draws below stay inside these ranges and needn't reach their ends.
Inputs may be any that keep to these rules, and one draw needn't show every extreme that they name: Each row of hist_lengths sums to 256; the tokens of a shard's users stand one after another in hist_ids.
All inputs are finite; a program needn't handle non-finite values.
Results may differ from the reference program's by a relative error of at most 0.015.
Values may be sent and summed in bfloat16 or wider, within the bound.
No kernel may reach another device: no remote copies, remote signals or barrier semaphores. Data moves between devices by JAX's collectives and lax.ppermute only.
A program may use at most 128 MiB of HBM per device.

```python
import math
import jax
import jax.numpy as jnp
import numpy as np
from jax import lax

D = 4096
FFW = 8448
HEADS = 16
HD = 128
NEG = 384
HT = 256
USERS_DEV = 16
LMAX = 64
ITEMS = 2048
N_USER = 16


def with_ends(values, stream_key, low, largest):
    shape = values.shape
    index_at = [jax.random.randint(jax.random.fold_in(stream_key, axis), (), 0, shape[axis]) for axis in range(len(shape))]
    values = values.at[tuple(index_at)].set(low)
    longest = shape.index(max(shape))
    index_at[longest] = (index_at[longest] + 1) % shape[longest]
    return values.at[tuple(index_at)].set(largest)


def levels(key, shape, shards, low, largest):
    def one(dim, blocks):
        steps = jax.random.uniform(jax.random.fold_in(jax.random.fold_in(key, 6), dim), (blocks,), jnp.float32, low / len(shards), largest / len(shards))
        return jnp.repeat(jnp.exp(steps), shape[dim] // blocks).reshape((-1,) + (1,) * (len(shape) - dim - 1))

    factor_of = one(*shards[0])
    for cut in shards[1:]:
        factor_of = factor_of * one(*cut)
    return factor_of


def cumulative_ranks(number_of, skew):
    portions = [(1 << 20) // math.isqrt(rank ** skew) + 1 for rank in range(1, number_of + 1)]
    scale = 1 + sum(portions) // (1 << 30)
    return np.cumsum(np.array([max(1, weight // scale) for weight in portions]))


def ranked(rng, extent, count, slope):
    listing = cumulative_ranks(count, slope)
    ticket = jax.random.randint(jax.random.fold_in(rng, 1), extent, 0, int(listing[count - 1]))
    standing = jnp.searchsorted(jnp.asarray(listing, jnp.int32), ticket, side="right")
    return jax.random.permutation(jax.random.fold_in(rng, 2), count)[standing].astype(jnp.int32)


def split_up(amount, total, reach, slope):
    loads = [(1 << 20) // math.isqrt(grade ** slope) + 1 for grade in range(2, amount + 1)]
    rest, given = total - reach - (amount - 1), [1] * (amount - 1)
    while rest > 0:
        candidates = [i for i in range(amount - 1) if given[i] < reach]
        pool, remaining = sum([loads[i] for i in candidates]), rest
        for i in candidates:
            addition = min(reach - given[i], max(1, remaining * loads[i] // pool), rest)
            given[i] = given[i] + addition
            rest = rest - addition
    return np.array([reach] + given)


def ragged(key, amount, total, most, slope):
    if amount == 2:
        one = jax.random.randint(key, (), max(1, total - most), min(most, total - 1) + 1)
        return jnp.stack([one, total - one])
    sizes = jnp.asarray(split_up(amount, total, most, slope), jnp.int32)
    couples = (amount - 1) // 2
    giver, sink = sizes[1:1 + 2 * couples:2], sizes[2:2 + 2 * couples:2]
    slack = jnp.minimum(giver - 1, most - sink)
    moved = jax.random.randint(jax.random.fold_in(key, 1), (couples,), 0, 1 << 20) % (slack + 1)
    sizes = sizes.at[1:1 + 2 * couples:2].set(giver - moved).at[2:2 + 2 * couples:2].set(sink + moved)
    return sizes[jax.random.permutation(jax.random.fold_in(key, 2), amount)]


def centred(stream_key, shape, width, bound, split=(), kind=jnp.bfloat16):
    values = jax.random.normal(stream_key, shape, jnp.float32) * width
    if len(split) > 0:
        values = levels(stream_key, shape, split, -0.22, 0.18) * values
    return jnp.clip(values, min=-bound, max=bound).astype(kind)


def setup_inputs(seed: int = 0) -> dict:
    streams_of = jax.random.split(jax.random.key(seed), 10)
    item_states = centred(streams_of[0], (ITEMS, D), 1.0, 6.0, ((0, 8), (1, 32)))
    w_gate = centred(streams_of[1], (D, FFW), D ** -0.5, 0.09375, ((1, 32),))
    w_up = centred(streams_of[2], (D, FFW), D ** -0.5, 0.09375, ((1, 32),))
    w_down = centred(streams_of[3], (FFW, D), FFW ** -0.5, 0.0625, ((0, 32),))
    w_qkv = centred(streams_of[4], (D, 3, HEADS * HD), D ** -0.5, 0.09375, ((2, 16),))
    w_out = centred(streams_of[5], (HEADS * HD, D), (HEADS * HD) ** -0.5, 0.125, ((0, 16),))
    hist_ids = with_ends(ranked(streams_of[6], (N_USER, HT), ITEMS, 2), jax.random.fold_in(streams_of[6], 3), 0, ITEMS - 1).astype(jnp.int32)
    hist_lengths = jax.vmap(lambda own: ragged(own, USERS_DEV, HT, LMAX, 2))(jax.random.split(streams_of[7], N_USER)).reshape((N_USER, USERS_DEV)).astype(jnp.int32)
    neg_ids = with_ends(jax.random.randint(streams_of[8], (N_USER, NEG), 0, ITEMS), jax.random.fold_in(streams_of[8], 1), 0, ITEMS - 1).astype(jnp.int32)
    return {"item_states": item_states, "w_gate": w_gate, "w_up": w_up, "w_down": w_down, "w_qkv": w_qkv, "w_out": w_out, "hist_ids": hist_ids, "hist_lengths": hist_lengths, "neg_ids": neg_ids}


masked_score = -1e30


def segment_of(lengths, seq_steps):
    user_ends = jnp.cumsum(lengths).astype(jnp.int32)
    position = jnp.arange(seq_steps, dtype=jnp.int32)
    return jnp.sum((position[:, None] >= user_ends[None, :]).astype(jnp.int32), axis=1).astype(jnp.int32)


def attend(states, w_qkv, segment):
    seq_steps = states.shape[0]
    head_width = w_qkv.shape[2]
    heads_here = head_width // HD
    projected = jnp.dot(states, w_qkv.reshape(D, 3 * head_width), preferred_element_type=jnp.float32).astype(jnp.bfloat16)
    projected = projected.reshape(seq_steps, 3, heads_here, HD).transpose(1, 2, 0, 3).astype(jnp.float32)
    scores = jnp.einsum("hqd,hkd->hqk", projected[0], projected[1]) * HD ** -0.5
    position = jnp.arange(seq_steps, dtype=jnp.int32)
    allowed = (segment[:, None] == segment[None, :]) & (position[:, None] >= position[None, :])
    scores = jnp.where(allowed[None], scores, masked_score)
    row_max = jnp.max(scores, axis=-1, keepdims=True)
    weights = jnp.exp(scores - row_max)
    weight_bf = (weights / jnp.sum(weights, axis=-1, keepdims=True)).astype(jnp.bfloat16)
    attended = jnp.einsum("hqk,hkd->hqd", weight_bf.astype(jnp.float32), projected[2]).astype(jnp.bfloat16)
    return attended.transpose(1, 0, 2).reshape(seq_steps, head_width)


def contrast(user_state, tokens, negatives, segment):
    logit_scale = D ** -0.5
    following = jnp.concatenate([tokens[1:], tokens[:1]], axis=0)
    user_wide = user_state.astype(jnp.float32)
    positive = jnp.sum(user_wide * following.astype(jnp.float32), axis=1) * logit_scale
    negative = jnp.einsum("td,nd->tn", user_wide, negatives.astype(jnp.float32)) * logit_scale
    usable = jnp.concatenate([segment[:-1] == segment[1:], jnp.zeros((1,), jnp.bool_)])
    row_max = jnp.maximum(positive, jnp.max(negative, axis=1))
    exp_total = jnp.exp(positive - row_max) + jnp.sum(jnp.exp(negative - row_max[:, None]), axis=1)
    return positive, negative, row_max + jnp.log(exp_total), usable


def reference(item_states, w_gate, w_up, w_down, w_qkv, w_out, hist_ids, hist_lengths, neg_ids):
    gate_sum = jnp.dot(item_states, w_gate, preferred_element_type=jnp.float32)
    up_sum = jnp.dot(item_states, w_up, preferred_element_type=jnp.float32)
    hidden = (jax.nn.silu(gate_sum) * up_sum).astype(jnp.bfloat16)
    item_emb = jnp.dot(hidden, w_down, preferred_element_type=jnp.float32).astype(jnp.bfloat16)
    pair_count = N_USER * (HT - USERS_DEV)
    shard_pairs = HT - USERS_DEV
    logit_scale = D ** -0.5

    def one_shard(grad_sum, inputs):
        hist_row, length_row, neg_row = inputs
        tokens = jnp.take(item_emb, hist_row, axis=0)
        negatives = jnp.take(item_emb, neg_row, axis=0)
        segment = segment_of(length_row, HT)
        attended = attend(tokens, w_qkv, segment)
        user_state = jnp.dot(attended, w_out, preferred_element_type=jnp.float32).astype(jnp.bfloat16)
        positive, negative, log_total, usable = contrast(user_state, tokens, negatives, segment)
        shard_loss = jnp.sum(jnp.where(usable, log_total - positive, 0.0)) / shard_pairs
        usable_f = usable.astype(jnp.float32) / pair_count
        pos_grad = (usable_f * (jnp.exp(positive - log_total) - 1.0)).astype(jnp.bfloat16)
        neg_grad = (usable_f[:, None] * jnp.exp(negative - log_total[:, None])).astype(jnp.bfloat16)
        user_wide = user_state.astype(jnp.float32)
        token_grad = jnp.concatenate([jnp.zeros((1, D), jnp.float32), pos_grad[:-1, None].astype(jnp.float32) * user_wide[:-1]], axis=0) * logit_scale
        negative_grad = jnp.dot(neg_grad.T, user_state, preferred_element_type=jnp.float32) * logit_scale
        grad_sum = grad_sum + jax.ops.segment_sum(token_grad, hist_row, num_segments=ITEMS)
        grad_sum = grad_sum + jax.ops.segment_sum(negative_grad, neg_row, num_segments=ITEMS)
        return grad_sum, (shard_loss.astype(jnp.float32), user_state)

    grad_sum, (loss, user_out) = lax.scan(one_shard, jnp.zeros((ITEMS, D), jnp.float32), (hist_ids, hist_lengths, neg_ids))
    return (loss, user_out, grad_sum)
```

```python
import functools

import jax
import jax.numpy as jnp
from jax import lax
from jax.experimental import pallas as pl
from jax.experimental.pallas import tpu as pltpu
from jax.sharding import PartitionSpec as P

D = 4096
HD = 128
LANE = 128

masked_score = -1e30
f32 = jnp.float32
bf16 = jnp.bfloat16

VMEM = pl.BlockSpec(memory_space=pltpu.VMEM)
SMEM = pl.BlockSpec(memory_space=pltpu.SMEM)


def call(kernel, out_shape, in_specs, args, scratch=(), vmem=32 << 20, flops=0, moved=0):
    many = isinstance(out_shape, tuple)
    return pl.pallas_call(
        kernel,
        out_shape=out_shape,
        in_specs=in_specs,
        out_specs=tuple(VMEM for _ in out_shape) if many else VMEM,
        scratch_shapes=list(scratch),
        compiler_params=pltpu.CompilerParams(vmem_limit_bytes=vmem),
        cost_estimate=pl.CostEstimate(flops=flops, bytes_accessed=moved, transcendentals=0),
    )(*args)


def dot(a, b):
    return jnp.dot(a, b, preferred_element_type=f32)


def dot_nt(a, b):
    return lax.dot_general(a, b, (((1,), (1,)), ((), ())), preferred_element_type=f32)


def dot_tn(a, b):
    return lax.dot_general(a, b, (((0,), (0,)), ((), ())), preferred_element_type=f32)


def aligned(start, unit):
    return pl.multiple_of(start, unit)


def ffn_kernel(tp_ref, mine_ref, other_ref, gate_ref, up_ref, down_ref, hidden_ref, send_ref, states_ref):
    tp = tp_ref[0]
    rows = hidden_ref.shape[0]
    chunks = mine_ref.shape[0]
    half = D // 2
    for u in range(chunks):
        base = u * (2 * LANE)
        states_ref[:, pl.ds(aligned(base + tp * LANE, LANE), LANE)] = mine_ref[u, :rows]
        states_ref[:, pl.ds(aligned(base + (1 - tp) * LANE, LANE), LANE)] = other_ref[u, :rows]
    gate = dot_nt(gate_ref[...], states_ref[...])
    up = dot_nt(up_ref[...], states_ref[...])
    hidden = jnp.transpose(gate / (1.0 + jnp.exp(-gate)) * up).astype(bf16)
    hidden_ref[...] = hidden
    part = dot(hidden, down_ref[:, pl.ds(aligned((1 - tp) * half, half), half)]).astype(bf16)
    for u in range(chunks):
        send_ref[u] = part[:, u * LANE : (u + 1) * LANE]


def down_kernel(tp_ref, hidden_ref, down_ref, got_ref, out_ref):
    half = D // 2
    part = dot(hidden_ref[...], down_ref[:, pl.ds(aligned(tp_ref[0] * half, half), half)])
    for u in range(out_ref.shape[0]):
        out_ref[u] = (part[:, u * LANE : (u + 1) * LANE] + got_ref[u].astype(f32)).astype(bf16)


def pick_kernel(ids_ref, emb_ref, out_ref):
    shards, rows = emb_ref.shape[0], emb_ref.shape[1]
    users, picks = out_ref.shape[0], out_ref.shape[1]
    items = emb_ref[...].reshape(shards * rows, LANE)
    slots = lax.broadcasted_iota(jnp.int32, (picks, rows), 1).astype(f32).astype(bf16)
    one, zero = jnp.ones((), bf16), jnp.zeros((), bf16)
    for u in range(users):
        ids = jnp.transpose(ids_ref[u])
        shard = jnp.broadcast_to(ids[:, 0:1], (picks, rows)).astype(bf16)
        slot = jnp.broadcast_to(ids[:, 1:2], (picks, rows)).astype(bf16)
        here = jnp.where(slot == slots, one, zero)
        select = jnp.concatenate([jnp.where(shard == k, here, zero) for k in range(shards)], axis=1)
        out_ref[u] = dot(select, items).astype(bf16)


def pick(ids, emb):
    users, picks = ids.shape[0], ids.shape[2]
    ids = jnp.concatenate([ids, jnp.zeros((users, 6, picks), f32)], axis=1)
    return call(
        pick_kernel,
        jax.ShapeDtypeStruct((users, picks, LANE), bf16),
        [VMEM, VMEM],
        (ids, emb),
        flops=2 * users * picks * emb.shape[1] * emb.shape[0] * LANE,
        moved=users * picks * LANE * 6,
    )


def project(half, tokens_ref, w_ref):
    rows = pl.ds(aligned(half * (D // 2), D // 2), D // 2)
    states = jnp.concatenate([tokens_ref[n] for n in range(tokens_ref.shape[0])], axis=1)
    return dot(states, jnp.concatenate([w_ref[j, rows, :] for j in range(3)], axis=1))


def project_kernel(half_ref, tokens_ref, w_ref, out_ref):
    out_ref[...] = project(half_ref[0], tokens_ref, w_ref)


def attend_kernel(half_ref, tokens_ref, w_ref, part_ref, allowed_ref, out_ref):
    projected = (part_ref[...] + project(half_ref[0], tokens_ref, w_ref)).astype(bf16)
    query, key, value = projected[:, :HD], projected[:, HD : 2 * HD], projected[:, 2 * HD :]
    scores = dot_nt(query, key) * HD ** (-0.5)
    scores = jnp.where(allowed_ref[...] > 0, scores, masked_score)
    weights = jnp.exp(scores - jnp.max(scores, axis=-1, keepdims=True))
    weights = (weights / jnp.sum(weights, axis=-1, keepdims=True)).astype(bf16)
    out_ref[...] = dot(weights, value).astype(bf16)


def cut_kernel(tp_ref, w_ref, keep_ref, send_ref):
    half = keep_ref.shape[1]
    keep_ref[...] = w_ref[:, pl.ds(aligned(tp_ref[0] * half, half), half)]
    send_ref[...] = w_ref[:, pl.ds(aligned((1 - tp_ref[0]) * half, half), half)]


def user_kernel(mine_ref, other_ref, w_ref, next_ref, neg_ref, user_ref, out_ref):
    shards, negs = mine_ref.shape[0], neg_ref.shape[1]
    parts = []
    for i in range(shards):
        parts += [mine_ref[i], other_ref[i]]
    heads = jnp.concatenate(parts, axis=1)
    user_ref[...] = dot(heads, w_ref[...].reshape(heads.shape[1], user_ref.shape[1])).astype(bf16)
    negatives = jnp.concatenate([neg_ref[u] for u in range(neg_ref.shape[0])], axis=1)
    out_ref[:, :negs] = dot_nt(user_ref[...], negatives)
    product = 0.0
    for u in range(next_ref.shape[0]):
        product += user_ref[:, u * LANE : (u + 1) * LANE].astype(f32) * next_ref[u].astype(f32)
    out_ref[:, negs:] = product


def grad_kernel(pairs, shard_pairs, near_ref, far_ref, usable_ref, next_ref, slot_ref, user_ref, loss_ref, out_ref):
    negs = slot_ref.shape[0]
    steps = near_ref.shape[0]
    rows = out_ref.shape[0]
    scale = D ** (-0.5)
    both = near_ref[...] + far_ref[...]
    negative = both[:, :negs] * scale
    positive = jnp.sum(both[:, negs:], axis=1, keepdims=True) * scale
    usable = usable_ref[...]
    row_max = jnp.maximum(positive, jnp.max(negative, axis=1, keepdims=True))
    exp_total = jnp.exp(positive - row_max) + jnp.sum(jnp.exp(negative - row_max), axis=1, keepdims=True)
    log_total = row_max + jnp.log(exp_total)
    loss = jnp.sum(jnp.where(usable > 0, log_total - positive, 0.0)) / shard_pairs
    loss_ref[...] = jnp.full(loss_ref.shape, loss, f32)
    usable_f = usable / pairs
    pos_grad = usable_f * (jnp.exp(positive - log_total) - 1.0)
    neg_grad = (usable_f * jnp.exp(negative - log_total)).astype(bf16)
    neg_pick = (slot_ref[...] == lax.broadcasted_iota(jnp.int32, (negs, rows), 1)).astype(f32).astype(bf16)
    pos_pick = next_ref[...] == lax.broadcasted_iota(jnp.int32, (steps, rows), 1)
    grad = (dot(neg_grad, neg_pick) + jnp.where(pos_pick, pos_grad, 0.0)).astype(bf16)
    out_ref[...] = (dot(jnp.transpose(grad), user_ref[...]) * scale).astype(bf16)


def segment_of(lengths, seq_steps):
    user_ends = jnp.cumsum(lengths)
    position = jnp.arange(seq_steps, dtype=jnp.int32)
    return jnp.sum((position[:, None] >= user_ends[None, :]).astype(jnp.int32), axis=1)


def exchange(x):
    return lax.ppermute(x, "tp", [(0, 1), (1, 0)])


def spread(x, axis):
    copies = jnp.broadcast_to(x[None], (lax.axis_size(axis),) + x.shape)
    return lax.all_to_all(copies, axis, 0, 0, tiled=True)


def ring(shards, shift):
    return [(i, (i + shift) % shards) for i in range(shards)]


def body(item_states, w_gate, w_up, w_down, w_qkv, w_out, hist_ids, hist_lengths, neg_ids):
    row_count = item_states.shape[0]
    users, shards = lax.axis_size("user"), lax.axis_size("item")
    half = D // 2
    tp = lax.axis_index("tp").astype(jnp.int32).reshape(1)
    hist_row, neg_row = hist_ids[0], neg_ids[0]
    seq_steps, negs = hist_row.shape[0], neg_row.shape[0]

    keep, send = call(
        cut_kernel,
        (jax.ShapeDtypeStruct((w_out.shape[0], half), bf16),) * 2,
        [SMEM, VMEM],
        (tp, w_out),
        moved=4 * w_out.shape[0] * D,
    )
    w_mix = lax.all_gather(jnp.stack([keep, exchange(send)]), "item", axis=0, tiled=False)

    named = jnp.concatenate([hist_row, neg_row])
    coded = jnp.stack([named // row_count, named % row_count]).reshape(-1, LANE)
    coded = jnp.pad(coded, ((0, -coded.shape[0] % 16), (0, 0))).astype(bf16)
    mine = spread(jnp.concatenate([item_states, coded], axis=0), "user")
    other = exchange(mine)
    all_ids = mine[:, row_count:].reshape(users, -1)[:, : 2 * (seq_steps + negs)].astype(f32)
    all_ids = all_ids.reshape(users, 2, seq_steps + negs)

    units = w_gate.shape[1]
    hidden, send = call(
        ffn_kernel,
        (
            jax.ShapeDtypeStruct((row_count, units), bf16),
            jax.ShapeDtypeStruct((users, row_count, LANE), bf16),
        ),
        [SMEM] + [VMEM] * 5,
        (tp, mine, other, w_gate.T, w_up.T, w_down),
        scratch=[pltpu.VMEM((row_count, D), bf16)],
        flops=5 * row_count * units * D,
        moved=6 * units * D,
    )
    got = exchange(send)
    partial = call(
        down_kernel,
        jax.ShapeDtypeStruct((users, row_count, LANE), bf16),
        [SMEM] + [VMEM] * 3,
        (tp, hidden, w_down, got),
        flops=row_count * units * D,
        moved=units * D,
    )
    partials = lax.all_to_all(partial, "user", 0, 0, tiled=True)
    emb = jnp.sum(partials.astype(f32), axis=0).astype(bf16)

    all_emb = spread(emb, "item")
    picked = pick(all_ids[:, :, :seq_steps], all_emb)
    picked, neg_ids_all = lax.optimization_barrier((picked, all_ids[:, :, seq_steps:]))
    picked_negatives = pick(neg_ids_all, all_emb)
    tokens = lax.all_to_all(picked, "user", 0, 0, tiled=True)
    tokens, picked_negatives = lax.optimization_barrier((tokens, picked_negatives))
    other_tokens = exchange(tokens)
    negatives = lax.all_to_all(picked_negatives, "user", 0, 0, tiled=True)

    segment = segment_of(hist_lengths[0], seq_steps)
    position = jnp.arange(seq_steps, dtype=jnp.int32)
    allowed = (segment[:, None] == segment[None, :]) & (position[:, None] >= position[None, :])
    allowed = allowed.astype(f32)
    qkv = w_qkv.transpose(1, 0, 2)
    qkv_width = qkv.shape[0] * qkv.shape[2]
    part = call(
        project_kernel,
        jax.ShapeDtypeStruct((seq_steps, qkv_width), f32),
        [SMEM] + [VMEM] * 2,
        (tp, tokens, qkv),
        flops=seq_steps * D * qkv_width,
        moved=D * qkv_width,
    )
    attended = call(
        attend_kernel,
        jax.ShapeDtypeStruct((seq_steps, HD), bf16),
        [SMEM] + [VMEM] * 4,
        (1 - tp, other_tokens, qkv, part, allowed),
        flops=seq_steps * D * qkv_width,
        moved=D * qkv_width,
    )
    item = lax.axis_index("item")
    heads = [attended] + [lax.ppermute(attended, "item", ring(shards, k)) for k in range(1, shards)]
    heads = jnp.stack(heads[::-1])
    heads = lax.dynamic_slice_in_dim(jnp.concatenate([heads, heads]), (shards - 1 - item) % shards, shards, 0)
    other_heads = exchange(heads)
    following = jnp.concatenate([tokens[:, 1:], tokens[:, :1]], axis=1)
    user_half, near = call(
        user_kernel,
        (
            jax.ShapeDtypeStruct((seq_steps, half), bf16),
            jax.ShapeDtypeStruct((seq_steps, negs + LANE), f32),
        ),
        [VMEM] * 5,
        (heads, other_heads, w_mix, following, negatives),
        flops=seq_steps * (negs + half) * D,
        moved=(negs + half) * D,
    )
    far = exchange(near)
    other_half = exchange(user_half)
    usable = jnp.concatenate([segment[:-1] == segment[1:], jnp.zeros((1,), jnp.bool_)]).astype(f32)
    shard_pairs = seq_steps - hist_lengths.shape[1]
    item_base = item.astype(jnp.int32) * row_count
    next_slot = jnp.concatenate([hist_row[1:], hist_row[:1]]) - item_base
    neg_slot = neg_row - item_base
    loss, item_part = call(
        functools.partial(grad_kernel, float(users * shard_pairs), float(shard_pairs)),
        (
            jax.ShapeDtypeStruct((8, LANE), f32),
            jax.ShapeDtypeStruct((row_count, half), bf16),
        ),
        [VMEM] * 6,
        (near, far, usable[:, None], next_slot[:, None], neg_slot[:, None], user_half),
        flops=2 * seq_steps * row_count * half,
        moved=row_count * half * 2,
    )
    parts = lax.all_to_all(item_part.reshape(users, row_count // users, half), "user", 0, 0, tiled=True)
    item_grad = jnp.sum(parts.astype(f32), axis=0)

    low = jnp.where(tp[0] == 0, user_half, other_half)
    high = jnp.where(tp[0] == 0, other_half, user_half)
    user_out = jnp.concatenate([low, high], axis=1)[None]
    return (loss[0, :1], user_out, item_grad)


def solution(mesh):
    placed = (
        P("item", ("user", "tp")),
        P(None, ("user", "tp")),
        P(None, ("user", "tp")),
        P(("user", "tp"), None),
        P(None, None, ("item", "tp")),
        P(("item", "tp"), None),
        P("user", None),
        P("user", None),
        P("user", None),
    )
    return jax.shard_map(
        body,
        mesh=mesh,
        in_specs=placed,
        out_specs=(P("user"), P("user", None, None), P(("item", "user"), "tp")),
        check_vma=False,
    )
```

```python
import functools

import jax
import jax.numpy as jnp
from jax import lax
from jax.experimental import pallas as pl
from jax.experimental.pallas import tpu as pltpu
from jax.sharding import PartitionSpec as P

D = 4096
HD = 128
LANE = 128

masked_score = -1e30
f32 = jnp.float32
bf16 = jnp.bfloat16

VMEM = pl.BlockSpec(memory_space=pltpu.VMEM)
SMEM = pl.BlockSpec(memory_space=pltpu.SMEM)
ANY = pl.BlockSpec(memory_space=pl.ANY)
HBM = pl.BlockSpec(memory_space=pltpu.HBM)
DMAS = pltpu.SemaphoreType.DMA


def call(kernel, out_shape, in_specs, args, scratch=(), out_specs=None, vmem=32 << 20, flops=0, moved=0):
    if out_specs is None:
        out_specs = tuple(VMEM for _ in out_shape) if isinstance(out_shape, tuple) else VMEM
    return pl.pallas_call(
        kernel,
        out_shape=out_shape,
        in_specs=in_specs,
        out_specs=out_specs,
        scratch_shapes=list(scratch),
        compiler_params=pltpu.CompilerParams(vmem_limit_bytes=vmem),
        cost_estimate=pl.CostEstimate(flops=flops, bytes_accessed=moved, transcendentals=0),
    )(*args)


def run(copies):
    for copy in copies:
        copy.start()
    for copy in copies:
        copy.wait()


def dot(a, b):
    return jnp.dot(a, b, preferred_element_type=f32)


def dot_nt(a, b):
    return lax.dot_general(a, b, (((1,), (1,)), ((), ())), preferred_element_type=f32)


def dot_tn(a, b):
    return lax.dot_general(a, b, (((0,), (0,)), ((), ())), preferred_element_type=f32)


def aligned(start, unit):
    return pl.multiple_of(start, unit)


def gate_up(first, states_ref, gate_ref, up_ref, rows):
    chunks = states_ref.shape[0]
    states = jnp.concatenate([states_ref[u, :rows] for u in range(chunks)], axis=1)

    def side(ref):
        blocks = [ref[:, pl.ds(aligned((2 * u + first) * LANE, LANE), LANE)] for u in range(chunks)]
        return dot_nt(jnp.concatenate(blocks, axis=1), states)

    return side(gate_ref), side(up_ref)


def ffn_near_kernel(tp_ref, mine_ref, gate_ref, up_ref, gate_out, up_out):
    gate_out[...], up_out[...] = gate_up(tp_ref[0], mine_ref, gate_ref, up_ref, gate_out.shape[1])


def ffn_kernel(tp_ref, other_ref, gate_near, up_near, gate_ref, up_ref, down_ref, hidden_ref, send_ref):
    tp = tp_ref[0]
    half = D // 2
    gate, up = gate_up(1 - tp, other_ref, gate_ref, up_ref, hidden_ref.shape[0])
    gate = gate_near[...] + gate
    up = up_near[...] + up
    hidden = jnp.transpose(gate / (1.0 + jnp.exp(-gate)) * up).astype(bf16)
    hidden_ref[...] = hidden
    part = dot(hidden, down_ref[:, pl.ds(aligned((1 - tp) * half, half), half)]).astype(bf16)
    for u in range(send_ref.shape[0]):
        send_ref[u] = part[:, u * LANE : (u + 1) * LANE]


def down_kernel(tp_ref, hidden_ref, down_ref, got_ref, out_ref):
    half = D // 2
    part = dot(hidden_ref[...], down_ref[:, pl.ds(aligned(tp_ref[0] * half, half), half)])
    for u in range(out_ref.shape[0]):
        out_ref[u] = (part[:, u * LANE : (u + 1) * LANE] + got_ref[u].astype(f32)).astype(bf16)


def pick_kernel(ids_ref, emb_ref, out_ref):
    shards, rows = emb_ref.shape[0], emb_ref.shape[1]
    users, picks = out_ref.shape[0], out_ref.shape[1]
    items = emb_ref[...].reshape(shards * rows, LANE)
    slots = lax.broadcasted_iota(jnp.int32, (picks, rows), 1).astype(f32).astype(bf16)
    one, zero = jnp.ones((), bf16), jnp.zeros((), bf16)
    for u in range(users):
        ids = jnp.transpose(ids_ref[u])
        shard = jnp.broadcast_to(ids[:, 0:1], (picks, rows)).astype(bf16)
        slot = jnp.broadcast_to(ids[:, 1:2], (picks, rows)).astype(bf16)
        here = jnp.where(slot == slots, one, zero)
        select = jnp.concatenate([jnp.where(shard == k, here, zero) for k in range(shards)], axis=1)
        out_ref[u] = dot(select, items).astype(bf16)


def pick(ids, emb):
    users, picks = ids.shape[0], ids.shape[2]
    ids = jnp.concatenate([ids, jnp.zeros((users, 6, picks), f32)], axis=1)
    return call(
        pick_kernel,
        jax.ShapeDtypeStruct((users, picks, LANE), bf16),
        [VMEM, VMEM],
        (ids, emb),
        flops=2 * users * picks * emb.shape[1] * emb.shape[0] * LANE,
        moved=users * picks * LANE * 6,
    )


def project(half, tokens_ref, w_ref):
    rows = pl.ds(aligned(half * (D // 2), D // 2), D // 2)
    states = jnp.concatenate([tokens_ref[n] for n in range(tokens_ref.shape[0])], axis=1)
    return dot(states, jnp.concatenate([w_ref[j, rows, :] for j in range(3)], axis=1))


def project_kernel(half_ref, tokens_ref, w_ref, out_ref):
    out_ref[...] = project(half_ref[0], tokens_ref, w_ref)


def attend_kernel(half_ref, tokens_ref, w_ref, part_ref, allowed_ref, out_ref):
    projected = (part_ref[...] + project(half_ref[0], tokens_ref, w_ref)).astype(bf16)
    query, key, value = projected[:, :HD], projected[:, HD : 2 * HD], projected[:, 2 * HD :]
    scores = dot_nt(query, key) * HD ** (-0.5)
    scores = jnp.where(allowed_ref[...] > 0, scores, masked_score)
    weights = jnp.exp(scores - jnp.max(scores, axis=-1, keepdims=True))
    weights = (weights / jnp.sum(weights, axis=-1, keepdims=True)).astype(bf16)
    out_ref[...] = dot(weights, value).astype(bf16)


def mix(half, heads, pieces, far, w_ref, sems):
    width = w_ref.shape[1]
    rows = w_ref.shape[0] // len(pieces)
    cols = pl.ds(aligned(half * width, width), width)
    copies = [
        pltpu.make_async_copy(piece.at[:, cols], w_ref.at[pl.ds(k * rows, rows)], sems.at[k])
        for k, piece in enumerate(pieces)
    ]
    for copy in copies:
        copy.start()
    total = 0.0
    group = len(heads) // 2
    for first in range(0, len(heads), group):
        for copy in copies[first : first + group]:
            copy.wait()
        states = jnp.concatenate([ref[...] for ref in heads[first : first + group]], axis=1)
        if first + group < len(heads):
            w = w_ref[first * rows : (first + group) * rows]
        else:
            last = [ref[:, cols] for ref in far]
            w = jnp.concatenate([w_ref[first * rows : (first + group - 1) * rows], *last], axis=0)
        total = total + dot(states, w)
    return total


def mix_kernel(shards, mine, tp_ref, *refs):
    heads, pieces, far = refs[:shards], refs[shards : 2 * shards - 1], refs[2 * shards - 1 : 2 * shards + 1]
    out_ref, w_ref, sems = refs[2 * shards + 1 :]
    half = tp_ref[0] if mine else 1 - tp_ref[0]
    out_ref[...] = mix(half, heads, pieces, far, w_ref, sems).astype(out_ref.dtype)


def user_kernel(own_ref, got_ref, token_ref, neg_ref, user_ref, out_ref):
    negs = neg_ref.shape[1]
    user_ref[...] = (own_ref[...] + got_ref[...].astype(f32)).astype(bf16)
    negatives = jnp.concatenate([neg_ref[u] for u in range(neg_ref.shape[0])], axis=1)
    out_ref[:, :negs] = dot_nt(user_ref[...], negatives)
    product = 0.0
    steps = token_ref.shape[1]
    for u in range(token_ref.shape[0]):
        following = pltpu.roll(token_ref[u].astype(f32), steps - 1, 0)
        product += user_ref[:, u * LANE : (u + 1) * LANE].astype(f32) * following
    out_ref[:, negs:] = product


def grad_kernel(
    pairs, shard_pairs, near_ref, far_ref, usable_ref, next_ref, slot_ref, user_ref, loss_ref, out_ref, buf, sems
):
    negs = slot_ref.shape[0]
    steps = near_ref.shape[0]
    rows = out_ref.shape[0]
    scale = D ** (-0.5)
    both = near_ref[...] + far_ref[...]
    negative = both[:, :negs] * scale
    positive = jnp.sum(both[:, negs:], axis=1, keepdims=True) * scale
    usable = usable_ref[...]
    row_max = jnp.maximum(positive, jnp.max(negative, axis=1, keepdims=True))
    exp_total = jnp.exp(positive - row_max) + jnp.sum(jnp.exp(negative - row_max), axis=1, keepdims=True)
    log_total = row_max + jnp.log(exp_total)
    loss = jnp.sum(jnp.where(usable > 0, log_total - positive, 0.0)) / shard_pairs
    loss_ref[...] = jnp.full(loss_ref.shape, loss, f32)
    usable_f = usable / pairs
    pos_grad = usable_f * (jnp.exp(positive - log_total) - 1.0)
    neg_grad = (usable_f * jnp.exp(negative - log_total)).astype(bf16)
    neg_pick = (slot_ref[...] == lax.broadcasted_iota(jnp.int32, (negs, rows), 1)).astype(f32).astype(bf16)
    pos_pick = next_ref[...] == lax.broadcasted_iota(jnp.int32, (steps, rows), 1)
    grad = (dot(neg_grad, neg_pick) + jnp.where(pos_pick, pos_grad, 0.0)).astype(bf16)
    grad = jnp.transpose(grad)
    copies = []
    block = rows // 2
    for n, first in enumerate(range(0, rows, block)):
        buf[first : first + block] = (dot(grad[first : first + block], user_ref[...]) * scale).astype(bf16)
        copies.append(
            pltpu.make_async_copy(buf.at[pl.ds(first, block)], out_ref.at[pl.ds(first, block)], sems.at[n])
        )
        copies[-1].start()
    for copy in copies:
        copy.wait()


def segment_of(lengths, seq_steps):
    user_ends = jnp.cumsum(lengths)
    position = jnp.arange(seq_steps, dtype=jnp.int32)
    return jnp.sum((position[:, None] >= user_ends[None, :]).astype(jnp.int32), axis=1)


def exchange(x):
    return lax.ppermute(x, "tp", [(0, 1), (1, 0)])


def spread(x, axis):
    copies = jnp.broadcast_to(x[None], (lax.axis_size(axis),) + x.shape)
    return lax.all_to_all(copies, axis, 0, 0, tiled=True)


def ring(shards, shift):
    return [(i, (i + shift) % shards) for i in range(shards)]


def body(item_states, w_gate, w_up, w_down, w_qkv, w_out, hist_ids, hist_lengths, neg_ids):
    row_count = item_states.shape[0]
    users, shards = lax.axis_size("user"), lax.axis_size("item")
    half = D // 2
    tp = lax.axis_index("tp").astype(jnp.int32).reshape(1)
    hist_row, neg_row = hist_ids[0], neg_ids[0]
    seq_steps, negs = hist_row.shape[0], neg_row.shape[0]

    right = functools.partial(lax.ppermute, axis_name="item", perm=ring(shards, 1))
    left = functools.partial(lax.ppermute, axis_name="item", perm=ring(shards, -1))
    pieces = [w_out, right(w_out), left(w_out)]

    named = jnp.concatenate([hist_row, neg_row])
    coded = jnp.stack([named // row_count, named % row_count]).reshape(-1, LANE)
    coded = jnp.pad(coded, ((0, -coded.shape[0] % 16), (0, 0))).astype(bf16)
    mine = spread(jnp.concatenate([item_states, coded], axis=0), "user")
    mine, *pieces[-2:] = lax.optimization_barrier((mine, *pieces[-2:]))
    pieces += [right(pieces[-2]), left(pieces[-1])]
    other = exchange(mine)
    all_ids = mine[:, row_count:].reshape(users, -1)[:, : 2 * (seq_steps + negs)].astype(f32)
    all_ids = all_ids.reshape(users, 2, seq_steps + negs)

    units = w_gate.shape[1]
    gate_near, up_near = call(
        ffn_near_kernel,
        (jax.ShapeDtypeStruct((units, row_count), f32),) * 2,
        [SMEM] + [VMEM] * 3,
        (tp, mine, w_gate.T, w_up.T),
        flops=2 * row_count * units * D,
        moved=4 * units * D,
    )
    hidden, send = call(
        ffn_kernel,
        (
            jax.ShapeDtypeStruct((row_count, units), bf16),
            jax.ShapeDtypeStruct((users, row_count, LANE), bf16),
        ),
        [SMEM] + [VMEM] * 6,
        (tp, other, gate_near, up_near, w_gate.T, w_up.T, w_down),
        flops=3 * row_count * units * D,
        moved=6 * units * D,
    )
    got = exchange(send)
    partial = call(
        down_kernel,
        jax.ShapeDtypeStruct((users, row_count, LANE), bf16),
        [SMEM] + [VMEM] * 3,
        (tp, hidden, w_down, got),
        flops=row_count * units * D,
        moved=units * D,
    )
    partials = lax.all_to_all(partial, "user", 0, 0, tiled=True)
    partials, *pieces[-2:] = lax.optimization_barrier((partials, *pieces[-2:]))
    pieces += [right(pieces[-2]), left(pieces[-1])]
    emb = jnp.sum(partials.astype(f32), axis=0).astype(bf16)

    all_emb = spread(emb, "item")
    picked = pick(all_ids[:, :, :seq_steps], all_emb)
    picked, neg_ids_all = lax.optimization_barrier((picked, all_ids[:, :, seq_steps:]))
    picked_negatives = pick(neg_ids_all, all_emb)
    tokens = lax.all_to_all(picked, "user", 0, 0, tiled=True)
    rows = w_out.shape[0] // 2
    ends = [pieces[-2][:rows], pieces[-1][rows:]]
    tokens, picked_negatives, *ends = lax.optimization_barrier((tokens, picked_negatives, *ends))
    far = [right(ends[0]), left(ends[1])]
    other_tokens = exchange(tokens)
    negatives = lax.all_to_all(picked_negatives, "user", 0, 0, tiled=True)

    segment = segment_of(hist_lengths[0], seq_steps)
    position = jnp.arange(seq_steps, dtype=jnp.int32)
    allowed = (segment[:, None] == segment[None, :]) & (position[:, None] >= position[None, :])
    allowed = allowed.astype(f32)
    qkv = w_qkv.transpose(1, 0, 2)
    qkv_width = qkv.shape[0] * qkv.shape[2]
    part = call(
        project_kernel,
        jax.ShapeDtypeStruct((seq_steps, qkv_width), f32),
        [SMEM] + [VMEM] * 2,
        (tp, tokens, qkv),
        flops=seq_steps * D * qkv_width,
        moved=D * qkv_width,
    )
    attended = call(
        attend_kernel,
        jax.ShapeDtypeStruct((seq_steps, HD), bf16),
        [SMEM] + [VMEM] * 4,
        (1 - tp, other_tokens, qkv, part, allowed),
        flops=seq_steps * D * qkv_width,
        moved=D * qkv_width,
    )
    shifts = [0, 1, -1, 2, -2, 3, -3, 4]
    heads = [attended] + [lax.ppermute(attended, "item", ring(shards, k)) for k in shifts[1:]]
    def mixed(mine):
        return call(
            functools.partial(mix_kernel, shards, mine),
            jax.ShapeDtypeStruct((seq_steps, half), f32 if mine else bf16),
            [SMEM] + [VMEM] * shards + [ANY] * (shards - 1) + [VMEM] * 2,
            [tp] + heads + pieces + far,
            scratch=[pltpu.VMEM(((shards - 1) * w_out.shape[0], half), bf16), DMAS((shards - 1,))],
            flops=seq_steps * half * D // 2,
            moved=half * D // 2,
        )

    got_user = exchange(mixed(False))
    own_user = mixed(True)
    user_half, near = call(
        user_kernel,
        (
            jax.ShapeDtypeStruct((seq_steps, half), bf16),
            jax.ShapeDtypeStruct((seq_steps, negs + LANE), f32),
        ),
        [VMEM] * 4,
        (own_user, got_user, tokens, negatives),
        flops=seq_steps * negs * D,
        moved=negs * D,
    )
    item = lax.axis_index("item")
    near_other = exchange(near)
    near_other, sent_half = lax.optimization_barrier((near_other, user_half))
    other_half = exchange(sent_half)
    usable = jnp.concatenate([segment[:-1] == segment[1:], jnp.zeros((1,), jnp.bool_)]).astype(f32)
    shard_pairs = seq_steps - hist_lengths.shape[1]
    item_base = item.astype(jnp.int32) * row_count
    next_slot = jnp.concatenate([hist_row[1:], hist_row[:1]]) - item_base
    neg_slot = neg_row - item_base
    loss, item_part = call(
        functools.partial(grad_kernel, float(users * shard_pairs), float(shard_pairs)),
        (
            jax.ShapeDtypeStruct((8, LANE), f32),
            jax.ShapeDtypeStruct((row_count, half), bf16),
        ),
        [VMEM] * 6,
        (near, near_other, usable[:, None], next_slot[:, None], neg_slot[:, None], user_half),
        scratch=[pltpu.VMEM((row_count, half), bf16), DMAS((2,))],
        out_specs=(VMEM, HBM),
        flops=2 * seq_steps * row_count * half,
        moved=row_count * half * 2,
    )
    parts = lax.all_to_all(item_part.reshape(users, row_count // users, half), "user", 0, 0, tiled=True)
    low = jnp.where(tp[0] == 0, user_half, other_half)
    high = jnp.where(tp[0] == 0, other_half, user_half)
    user_out = jnp.concatenate([low, high], axis=1)[None]
    parts, user_out = lax.optimization_barrier((parts, user_out))
    item_grad = jnp.sum(parts.astype(f32), axis=0)
    return (loss[0, :1], user_out, item_grad)


def solution(mesh):
    placed = (
        P("item", ("user", "tp")),
        P(None, ("user", "tp")),
        P(None, ("user", "tp")),
        P(("user", "tp"), None),
        P(None, None, ("item", "tp")),
        P(("item", "tp"), None),
        P("user", None),
        P("user", None),
        P("user", None),
    )
    return jax.shard_map(
        body,
        mesh=mesh,
        in_specs=placed,
        out_specs=(P("user"), P("user", None, None), P(("item", "user"), "tp")),
        check_vma=False,
    )
```

```python
import functools

import jax
import jax.numpy as jnp
from jax import lax
from jax.experimental import pallas as pl
from jax.experimental.pallas import tpu as pltpu
from jax.sharding import PartitionSpec as P

D = 4096
HD = 128
LANE = 128

masked_score = -1e30
f32 = jnp.float32
bf16 = jnp.bfloat16

VMEM = pl.BlockSpec(memory_space=pltpu.VMEM)
SMEM = pl.BlockSpec(memory_space=pltpu.SMEM)
ANY = pl.BlockSpec(memory_space=pl.ANY)
HBM = pl.BlockSpec(memory_space=pltpu.HBM)
DMAS = pltpu.SemaphoreType.DMA


def call(kernel, out_shape, in_specs, args, scratch=(), out_specs=None, vmem=12 << 20, flops=0, moved=0):
    if out_specs is None:
        out_specs = tuple(VMEM for _ in out_shape) if isinstance(out_shape, tuple) else VMEM
    return pl.pallas_call(
        kernel,
        out_shape=out_shape,
        in_specs=in_specs,
        out_specs=out_specs,
        scratch_shapes=list(scratch),
        compiler_params=pltpu.CompilerParams(vmem_limit_bytes=vmem),
        cost_estimate=pl.CostEstimate(flops=flops, bytes_accessed=moved, transcendentals=0),
    )(*args)


def run(copies):
    for copy in copies:
        copy.start()
    for copy in copies:
        copy.wait()


def dot(a, b):
    return jnp.dot(a, b, preferred_element_type=f32)


def dot_nt(a, b):
    return lax.dot_general(a, b, (((1,), (1,)), ((), ())), preferred_element_type=f32)


def dot_tn(a, b):
    return lax.dot_general(a, b, (((0,), (0,)), ((), ())), preferred_element_type=f32)


def aligned(start, unit):
    return pl.multiple_of(start, unit)


def gate_up(first, states_ref, gate_ref, up_ref, rows):
    chunks = states_ref.shape[0]
    states = jnp.concatenate([states_ref[u, :rows] for u in range(chunks)], axis=1)

    def side(ref):
        blocks = [ref[:, pl.ds(aligned((2 * u + first) * LANE, LANE), LANE)] for u in range(chunks)]
        return dot_nt(jnp.concatenate(blocks, axis=1), states)

    return side(gate_ref), side(up_ref)


def ffn_near_kernel(tp_ref, mine_ref, gate_ref, up_ref, gate_out, up_out):
    gate_out[...], up_out[...] = gate_up(tp_ref[0], mine_ref, gate_ref, up_ref, gate_out.shape[1])


def ffn_kernel(tp_ref, other_ref, gate_near, up_near, gate_ref, up_ref, down_ref, hidden_ref, send_ref):
    tp = tp_ref[0]
    half = D // 2
    gate, up = gate_up(1 - tp, other_ref, gate_ref, up_ref, hidden_ref.shape[0])
    gate = gate_near[...] + gate
    up = up_near[...] + up
    hidden = jnp.transpose(gate / (1.0 + jnp.exp(-gate)) * up).astype(bf16)
    hidden_ref[...] = hidden
    part = dot(hidden, down_ref[:, pl.ds(aligned((1 - tp) * half, half), half)]).astype(bf16)
    for u in range(send_ref.shape[0]):
        send_ref[u] = part[:, u * LANE : (u + 1) * LANE]


def down_kernel(tp_ref, hidden_ref, down_ref, got_ref, out_ref):
    half = D // 2
    part = dot(hidden_ref[...], down_ref[:, pl.ds(aligned(tp_ref[0] * half, half), half)])
    for u in range(out_ref.shape[0]):
        out_ref[u] = (part[:, u * LANE : (u + 1) * LANE] + got_ref[u].astype(f32)).astype(bf16)


def pick_kernel(ids_ref, emb_ref, out_ref):
    shards, rows = emb_ref.shape[0], emb_ref.shape[1]
    users, picks = out_ref.shape[0], out_ref.shape[1]
    group = shards // 2
    sides = [emb_ref[n * group : (n + 1) * group].reshape(group * rows, LANE) for n in range(2)]
    items = jnp.concatenate(sides, axis=1)
    slots = lax.broadcasted_iota(jnp.int32, (picks, rows), 1).astype(f32).astype(bf16)
    one, zero = jnp.ones((), bf16), jnp.zeros((), bf16)
    for u in range(users):
        ids = jnp.transpose(ids_ref[u])
        upper = ids[:, 0:1] >= group
        shard = jnp.broadcast_to(jnp.where(upper, ids[:, 0:1] - group, ids[:, 0:1]), (picks, rows)).astype(bf16)
        slot = jnp.broadcast_to(ids[:, 1:2], (picks, rows)).astype(bf16)
        here = jnp.where(slot == slots, one, zero)
        select = jnp.concatenate([jnp.where(shard == k, here, zero) for k in range(group)], axis=1)
        found = dot(select, items)
        out_ref[u] = jnp.where(upper, found[:, LANE:], found[:, :LANE]).astype(bf16)


def pick(ids, emb):
    users, picks = ids.shape[0], ids.shape[2]
    ids = jnp.concatenate([ids, jnp.zeros((users, 6, picks), f32)], axis=1)
    return call(
        pick_kernel,
        jax.ShapeDtypeStruct((users, picks, LANE), bf16),
        [VMEM, VMEM],
        (ids, emb),
        flops=2 * users * picks * emb.shape[1] * emb.shape[0] * LANE,
        moved=users * picks * LANE * 6,
    )


def project(half, tokens_ref, w_ref):
    rows = pl.ds(aligned(half * (D // 2), D // 2), D // 2)
    states = jnp.concatenate([tokens_ref[n] for n in range(tokens_ref.shape[0])], axis=1)
    return dot(states, jnp.concatenate([w_ref[j, rows, :] for j in range(3)], axis=1))


def project_kernel(half_ref, tokens_ref, w_ref, out_ref):
    out_ref[...] = project(half_ref[0], tokens_ref, w_ref)


def attend_kernel(half_ref, tokens_ref, w_ref, part_ref, allowed_ref, out_ref):
    projected = (part_ref[...] + project(half_ref[0], tokens_ref, w_ref)).astype(bf16)
    query, key, value = projected[:, :HD], projected[:, HD : 2 * HD], projected[:, 2 * HD :]
    scores = dot_nt(query, key) * HD ** (-0.5)
    scores = jnp.where(allowed_ref[...] > 0, scores, masked_score)
    weights = jnp.exp(scores - jnp.max(scores, axis=-1, keepdims=True))
    weights = (weights / jnp.sum(weights, axis=-1, keepdims=True)).astype(bf16)
    out_ref[...] = dot(weights, value).astype(bf16)


def fetch_kernel(shards, tp_ref, *refs):
    pieces, far, outs, sems = refs[: shards - 1], refs[shards - 1 : shards + 1], refs[shards + 1 : -1], refs[-1]
    width = outs[0].shape[1]
    rows = outs[0].shape[0] // shards
    copies = []
    for n, out_ref in enumerate(outs):
        half = tp_ref[0] if n else 1 - tp_ref[0]
        cols = pl.ds(aligned(half * width, width), width)
        for k, piece in enumerate(pieces):
            copies.append((piece.at[:, cols], out_ref.at[pl.ds(k * rows, rows)]))
        for k, piece in enumerate(far):
            first = (shards - 1) * rows + k * (rows // 2)
            copies.append((piece.at[:, cols], out_ref.at[pl.ds(first, rows // 2)]))
    run([pltpu.make_async_copy(src, dst, sems.at[n]) for n, (src, dst) in enumerate(copies)])


def mix_kernel(shards, *refs):
    heads, (w_ref, out_ref) = refs[:shards], refs[shards:]
    states = jnp.concatenate([ref[...] for ref in heads], axis=1)
    out_ref[...] = dot(states, w_ref[...]).astype(out_ref.dtype)


def user_kernel(own_ref, got_ref, token_ref, neg_ref, user_ref, out_ref):
    negs = neg_ref.shape[1]
    user_ref[...] = (own_ref[...] + got_ref[...].astype(f32)).astype(bf16)
    negatives = jnp.concatenate([neg_ref[u] for u in range(neg_ref.shape[0])], axis=1)
    out_ref[:, :negs] = dot_nt(user_ref[...], negatives)
    product = 0.0
    steps = token_ref.shape[1]
    for u in range(token_ref.shape[0]):
        following = pltpu.roll(token_ref[u].astype(f32), steps - 1, 0)
        product += user_ref[:, u * LANE : (u + 1) * LANE].astype(f32) * following
    out_ref[:, negs:] = product


def grad_kernel(
    pairs, shard_pairs, near_ref, far_ref, usable_ref, next_ref, slot_ref, user_ref, loss_ref, out_ref, buf, sems
):
    negs = slot_ref.shape[0]
    steps = near_ref.shape[0]
    rows = out_ref.shape[0]
    scale = D ** (-0.5)
    both = near_ref[...] + far_ref[...]
    negative = both[:, :negs] * scale
    positive = jnp.sum(both[:, negs:], axis=1, keepdims=True) * scale
    usable = usable_ref[...]
    row_max = jnp.maximum(positive, jnp.max(negative, axis=1, keepdims=True))
    exp_total = jnp.exp(positive - row_max) + jnp.sum(jnp.exp(negative - row_max), axis=1, keepdims=True)
    log_total = row_max + jnp.log(exp_total)
    loss = jnp.sum(jnp.where(usable > 0, log_total - positive, 0.0)) / shard_pairs
    loss_ref[...] = jnp.full(loss_ref.shape, loss, f32)
    usable_f = usable / pairs
    pos_grad = usable_f * (jnp.exp(positive - log_total) - 1.0)
    neg_grad = (usable_f * jnp.exp(negative - log_total)).astype(bf16)
    neg_pick = (slot_ref[...] == lax.broadcasted_iota(jnp.int32, (negs, rows), 1)).astype(f32).astype(bf16)
    pos_pick = next_ref[...] == lax.broadcasted_iota(jnp.int32, (steps, rows), 1)
    grad = (dot(neg_grad, neg_pick) + jnp.where(pos_pick, pos_grad, 0.0)).astype(bf16)
    grad = jnp.transpose(grad)
    copies = []
    block = rows // 2
    for n, first in enumerate(range(0, rows, block)):
        buf[first : first + block] = (dot(grad[first : first + block], user_ref[...]) * scale).astype(bf16)
        copies.append(
            pltpu.make_async_copy(buf.at[pl.ds(first, block)], out_ref.at[pl.ds(first, block)], sems.at[n])
        )
        copies[-1].start()
    for copy in copies:
        copy.wait()


def segment_of(lengths, seq_steps):
    user_ends = jnp.cumsum(lengths)
    position = jnp.arange(seq_steps, dtype=jnp.int32)
    return jnp.sum((position[:, None] >= user_ends[None, :]).astype(jnp.int32), axis=1)


def exchange(x):
    return lax.ppermute(x, "tp", [(0, 1), (1, 0)])


def spread(x, axis):
    copies = jnp.broadcast_to(x[None], (lax.axis_size(axis),) + x.shape)
    return lax.all_to_all(copies, axis, 0, 0, tiled=True)


def ring(shards, shift):
    return [(i, (i + shift) % shards) for i in range(shards)]


def body(item_states, w_gate, w_up, w_down, w_qkv, w_out, hist_ids, hist_lengths, neg_ids):
    row_count = item_states.shape[0]
    users, shards = lax.axis_size("user"), lax.axis_size("item")
    half = D // 2
    tp = lax.axis_index("tp").astype(jnp.int32).reshape(1)
    hist_row, neg_row = hist_ids[0], neg_ids[0]
    seq_steps, negs = hist_row.shape[0], neg_row.shape[0]

    right = functools.partial(lax.ppermute, axis_name="item", perm=ring(shards, 1))
    left = functools.partial(lax.ppermute, axis_name="item", perm=ring(shards, -1))
    pieces = [w_out, right(w_out), left(w_out)]

    named = jnp.concatenate([hist_row, neg_row])
    coded = jnp.stack([named // row_count, named % row_count]).reshape(-1, LANE)
    coded = jnp.pad(coded, ((0, -coded.shape[0] % 16), (0, 0))).astype(bf16)
    mine = spread(jnp.concatenate([item_states, coded], axis=0), "user")
    mine, *pieces[-2:] = lax.optimization_barrier((mine, *pieces[-2:]))
    pieces += [right(pieces[-2]), left(pieces[-1])]
    other = exchange(mine)
    all_ids = mine[:, row_count:].reshape(users, -1)[:, : 2 * (seq_steps + negs)].astype(f32)
    all_ids = all_ids.reshape(users, 2, seq_steps + negs)

    units = w_gate.shape[1]
    gate_near, up_near = call(
        ffn_near_kernel,
        (jax.ShapeDtypeStruct((units, row_count), f32),) * 2,
        [SMEM] + [VMEM] * 3,
        (tp, mine, w_gate.T, w_up.T),
        flops=2 * row_count * units * D,
        moved=4 * units * D,
    )
    hidden, send = call(
        ffn_kernel,
        (
            jax.ShapeDtypeStruct((row_count, units), bf16),
            jax.ShapeDtypeStruct((users, row_count, LANE), bf16),
        ),
        [SMEM] + [VMEM] * 6,
        (tp, other, gate_near, up_near, w_gate.T, w_up.T, w_down),
        flops=3 * row_count * units * D,
        moved=6 * units * D,
    )
    got = exchange(send)
    partial = call(
        down_kernel,
        jax.ShapeDtypeStruct((users, row_count, LANE), bf16),
        [SMEM] + [VMEM] * 3,
        (tp, hidden, w_down, got),
        flops=row_count * units * D,
        moved=units * D,
    )
    partials = lax.all_to_all(partial, "user", 0, 0, tiled=True)
    partials, *pieces[-2:] = lax.optimization_barrier((partials, *pieces[-2:]))
    pieces += [right(pieces[-2]), left(pieces[-1])]
    emb = jnp.sum(partials.astype(f32), axis=0).astype(bf16)

    all_emb = spread(emb, "item")
    picked = pick(all_ids[:, :, :seq_steps], all_emb)
    picked, neg_ids_all = lax.optimization_barrier((picked, all_ids[:, :, seq_steps:]))
    picked_negatives = pick(neg_ids_all, all_emb)
    tokens = lax.all_to_all(picked, "user", 0, 0, tiled=True)
    segment = segment_of(hist_lengths[0], seq_steps)
    position = jnp.arange(seq_steps, dtype=jnp.int32)
    allowed = (segment[:, None] == segment[None, :]) & (position[:, None] >= position[None, :])
    allowed = allowed.astype(f32)
    usable = jnp.concatenate([segment[:-1] == segment[1:], jnp.zeros((1,), jnp.bool_)]).astype(f32)[:, None]
    item_base = lax.axis_index("item").astype(jnp.int32) * row_count
    next_slot = (jnp.concatenate([hist_row[1:], hist_row[:1]]) - item_base)[:, None]
    neg_slot = (neg_row - item_base)[:, None]
    rows = w_out.shape[0] // 2
    ends = [pieces[-2][:rows], pieces[-1][rows:]]
    masks = (allowed, usable, next_slot, neg_slot)
    tokens, picked_negatives, ends, masks = lax.optimization_barrier((tokens, picked_negatives, ends, masks))
    allowed, usable, next_slot, neg_slot = masks
    far = [right(ends[0]), left(ends[1])]
    other_tokens = exchange(tokens)
    negatives = lax.all_to_all(picked_negatives, "user", 0, 0, tiled=True)

    qkv = w_qkv.transpose(1, 0, 2)
    qkv_width = qkv.shape[0] * qkv.shape[2]
    part = call(
        project_kernel,
        jax.ShapeDtypeStruct((seq_steps, qkv_width), f32),
        [SMEM] + [VMEM] * 2,
        (tp, tokens, qkv),
        flops=seq_steps * D * qkv_width,
        moved=D * qkv_width,
    )
    attended = call(
        attend_kernel,
        jax.ShapeDtypeStruct((seq_steps, HD), bf16),
        [SMEM] + [VMEM] * 4,
        (1 - tp, other_tokens, qkv, part, allowed),
        flops=seq_steps * D * qkv_width,
        moved=D * qkv_width,
    )
    shifts = [0, 1, -1, 2, -2, 3, -3, 4]
    heads = [attended] + [lax.ppermute(attended, "item", ring(shards, k)) for k in shifts[1:]]
    w_send, w_keep = call(
        functools.partial(fetch_kernel, shards),
        (jax.ShapeDtypeStruct((shards * w_out.shape[0], half), bf16),) * 2,
        [SMEM] + [ANY] * (shards + 1),
        [tp] + pieces + far,
        scratch=[DMAS((2 * shards + 2,))],
        moved=4 * shards * w_out.shape[0] * D,
    )

    def mixed(w, kind):
        return call(
            functools.partial(mix_kernel, shards),
            jax.ShapeDtypeStruct((seq_steps, half), kind),
            [VMEM] * (shards + 1),
            heads + [w],
            flops=seq_steps * half * D // 2,
            moved=half * D // 2,
        )

    got_user = exchange(mixed(w_send, bf16))
    own_user = mixed(w_keep, f32)
    user_half, near = call(
        user_kernel,
        (
            jax.ShapeDtypeStruct((seq_steps, half), bf16),
            jax.ShapeDtypeStruct((seq_steps, negs + LANE), f32),
        ),
        [VMEM] * 4,
        (own_user, got_user, tokens, negatives),
        flops=seq_steps * negs * D,
        moved=negs * D,
    )
    near_other = exchange(near)
    near_other, sent_half = lax.optimization_barrier((near_other, user_half))
    other_half = exchange(sent_half)
    shard_pairs = seq_steps - hist_lengths.shape[1]
    loss, item_part = call(
        functools.partial(grad_kernel, float(users * shard_pairs), float(shard_pairs)),
        (
            jax.ShapeDtypeStruct((8, LANE), f32),
            jax.ShapeDtypeStruct((row_count, half), bf16),
        ),
        [VMEM] * 6,
        (near, near_other, usable, next_slot, neg_slot, user_half),
        scratch=[pltpu.VMEM((row_count, half), bf16), DMAS((2,))],
        out_specs=(VMEM, HBM),
        flops=2 * seq_steps * row_count * half,
        moved=row_count * half * 2,
    )
    parts = lax.all_to_all(item_part.reshape(users, row_count // users, half), "user", 0, 0, tiled=True)
    low = jnp.where(tp[0] == 0, user_half, other_half)
    high = jnp.where(tp[0] == 0, other_half, user_half)
    user_out = jnp.concatenate([low, high], axis=1)[None]
    parts, user_out = lax.optimization_barrier((parts, user_out))
    item_grad = jnp.sum(parts.astype(f32), axis=0)
    return (loss[0, :1], user_out, item_grad)


def solution(mesh):
    placed = (
        P("item", ("user", "tp")),
        P(None, ("user", "tp")),
        P(None, ("user", "tp")),
        P(("user", "tp"), None),
        P(None, None, ("item", "tp")),
        P(("item", "tp"), None),
        P("user", None),
        P("user", None),
        P("user", None),
    )
    return jax.shard_map(
        body,
        mesh=mesh,
        in_specs=placed,
        out_specs=(P("user"), P("user", None, None), P(("item", "user"), "tp")),
        check_vma=False,
    )
```

```python
import functools

import jax
import jax.numpy as jnp
from jax import lax
from jax.experimental import pallas as pl
from jax.experimental.pallas import tpu as pltpu
from jax.sharding import PartitionSpec as P

D = 4096
HD = 128
LANE = 128

masked_score = -1e30
f32 = jnp.float32
bf16 = jnp.bfloat16

VMEM = pl.BlockSpec(memory_space=pltpu.VMEM)
SMEM = pl.BlockSpec(memory_space=pltpu.SMEM)
ANY = pl.BlockSpec(memory_space=pl.ANY)
HBM = pl.BlockSpec(memory_space=pltpu.HBM)
DMAS = pltpu.SemaphoreType.DMA


def call(kernel, out_shape, in_specs, args, scratch=(), out_specs=None, vmem=12 << 20, flops=0, moved=0):
    if out_specs is None:
        out_specs = tuple(VMEM for _ in out_shape) if isinstance(out_shape, tuple) else VMEM
    return pl.pallas_call(
        kernel,
        out_shape=out_shape,
        in_specs=in_specs,
        out_specs=out_specs,
        scratch_shapes=list(scratch),
        compiler_params=pltpu.CompilerParams(vmem_limit_bytes=vmem),
        cost_estimate=pl.CostEstimate(flops=flops, bytes_accessed=moved, transcendentals=0),
    )(*args)


def run(copies):
    for copy in copies:
        copy.start()
    for copy in copies:
        copy.wait()


def dot(a, b):
    return jnp.dot(a, b, preferred_element_type=f32)


def dot_nt(a, b):
    return lax.dot_general(a, b, (((1,), (1,)), ((), ())), preferred_element_type=f32)


def dot_tn(a, b):
    return lax.dot_general(a, b, (((0,), (0,)), ((), ())), preferred_element_type=f32)


def aligned(start, unit):
    return pl.multiple_of(start, unit)


def gate_up(first, states_ref, gate_ref, up_ref, rows):
    chunks = states_ref.shape[0]
    states = jnp.concatenate([states_ref[u, :rows] for u in range(chunks)], axis=1)

    def side(ref):
        blocks = [ref[:, pl.ds(aligned((2 * u + first) * LANE, LANE), LANE)] for u in range(chunks)]
        return dot_nt(jnp.concatenate(blocks, axis=1), states)

    return side(gate_ref), side(up_ref)


def ffn_near_kernel(tp_ref, mine_ref, gate_ref, up_ref, gate_out, up_out):
    gate_out[...], up_out[...] = gate_up(tp_ref[0], mine_ref, gate_ref, up_ref, gate_out.shape[1])


def ffn_kernel(tp_ref, other_ref, gate_near, up_near, gate_ref, up_ref, down_ref, hidden_ref, send_ref):
    tp = tp_ref[0]
    half = D // 2
    gate, up = gate_up(1 - tp, other_ref, gate_ref, up_ref, hidden_ref.shape[0])
    gate = gate_near[...] + gate
    up = up_near[...] + up
    hidden = jnp.transpose(gate / (1.0 + jnp.exp(-gate)) * up).astype(bf16)
    hidden_ref[...] = hidden
    part = dot(hidden, down_ref[:, pl.ds(aligned((1 - tp) * half, half), half)]).astype(bf16)
    for u in range(send_ref.shape[0]):
        send_ref[u] = part[:, u * LANE : (u + 1) * LANE]


def down_kernel(tp_ref, hidden_ref, down_ref, got_ref, out_ref):
    half = D // 2
    part = dot(hidden_ref[...], down_ref[:, pl.ds(aligned(tp_ref[0] * half, half), half)])
    for u in range(out_ref.shape[0]):
        out_ref[u] = (part[:, u * LANE : (u + 1) * LANE] + got_ref[u].astype(f32)).astype(bf16)


def pick_kernel(ids_ref, emb_ref, out_ref):
    shards, rows = emb_ref.shape[0], emb_ref.shape[1]
    users, picks = out_ref.shape[0], out_ref.shape[1]
    group = shards // 2
    sides = [emb_ref[n * group : (n + 1) * group].reshape(group * rows, LANE) for n in range(2)]
    items = jnp.concatenate(sides, axis=1)
    slots = lax.broadcasted_iota(jnp.int32, (picks, rows), 1).astype(f32).astype(bf16)
    one, zero = jnp.ones((), bf16), jnp.zeros((), bf16)
    for u in range(users):
        ids = jnp.transpose(ids_ref[u])
        upper = ids[:, 0:1] >= group
        shard = jnp.broadcast_to(jnp.where(upper, ids[:, 0:1] - group, ids[:, 0:1]), (picks, rows)).astype(bf16)
        slot = jnp.broadcast_to(ids[:, 1:2], (picks, rows)).astype(bf16)
        here = jnp.where(slot == slots, one, zero)
        select = jnp.concatenate([jnp.where(shard == k, here, zero) for k in range(group)], axis=1)
        found = dot(select, items)
        out_ref[u] = jnp.where(upper, found[:, LANE:], found[:, :LANE]).astype(bf16)


def pick(ids, emb):
    users, picks = ids.shape[0], ids.shape[2]
    ids = jnp.concatenate([ids, jnp.zeros((users, 6, picks), f32)], axis=1)
    return call(
        pick_kernel,
        jax.ShapeDtypeStruct((users, picks, LANE), bf16),
        [VMEM, VMEM],
        (ids, emb),
        flops=2 * users * picks * emb.shape[1] * emb.shape[0] * LANE,
        moved=users * picks * LANE * 6,
    )


def project(half, tokens_ref, w_ref):
    rows = pl.ds(aligned(half * (D // 2), D // 2), D // 2)
    states = jnp.concatenate([tokens_ref[n] for n in range(tokens_ref.shape[0])], axis=1)
    return dot(states, jnp.concatenate([w_ref[j, rows, :] for j in range(3)], axis=1))


def project_kernel(half_ref, tokens_ref, w_ref, out_ref):
    out_ref[...] = project(half_ref[0], tokens_ref, w_ref)


def attend_kernel(half_ref, tokens_ref, w_ref, part_ref, allowed_ref, out_ref):
    projected = (part_ref[...] + project(half_ref[0], tokens_ref, w_ref)).astype(bf16)
    query, key, value = projected[:, :HD], projected[:, HD : 2 * HD], projected[:, 2 * HD :]
    scores = dot_nt(query, key) * HD ** (-0.5)
    scores = jnp.where(allowed_ref[...] > 0, scores, masked_score)
    weights = jnp.exp(scores - jnp.max(scores, axis=-1, keepdims=True))
    weights = (weights / jnp.sum(weights, axis=-1, keepdims=True)).astype(bf16)
    out_ref[...] = dot(weights, value).astype(bf16)


def fetch_kernel(shards, tp_ref, *refs):
    pieces, far, outs, sems = refs[: shards - 1], refs[shards - 1 : shards + 1], refs[shards + 1 : -1], refs[-1]
    width = outs[0].shape[1]
    rows = outs[0].shape[0] // shards
    copies = []
    for n, out_ref in enumerate(outs):
        half = tp_ref[0] if n else 1 - tp_ref[0]
        cols = pl.ds(aligned(half * width, width), width)
        for k, piece in enumerate(pieces):
            copies.append((piece.at[:, cols], out_ref.at[pl.ds(k * rows, rows)]))
        for k, piece in enumerate(far):
            first = (shards - 1) * rows + k * (rows // 2)
            copies.append((piece.at[:, cols], out_ref.at[pl.ds(first, rows // 2)]))
    run([pltpu.make_async_copy(src, dst, sems.at[n]) for n, (src, dst) in enumerate(copies)])


def mix_kernel(shards, *refs):
    heads, (w_ref, out_ref) = refs[:shards], refs[shards:]
    states = jnp.concatenate([ref[...] for ref in heads], axis=1)
    out_ref[...] = dot(states, w_ref[...]).astype(out_ref.dtype)


def user_kernel(own_ref, got_ref, token_ref, neg_ref, user_ref, out_ref):
    negs = neg_ref.shape[1]
    user_ref[...] = (own_ref[...] + got_ref[...].astype(f32)).astype(bf16)
    negatives = jnp.concatenate([neg_ref[u] for u in range(neg_ref.shape[0])], axis=1)
    out_ref[:, :negs] = dot_nt(user_ref[...], negatives)
    product = 0.0
    steps = token_ref.shape[1]
    for u in range(token_ref.shape[0]):
        following = pltpu.roll(token_ref[u].astype(f32), steps - 1, 0)
        product += user_ref[:, u * LANE : (u + 1) * LANE].astype(f32) * following
    out_ref[:, negs:] = product


def grad_kernel(
    pairs, shard_pairs, near_ref, far_ref, usable_ref, next_ref, slot_ref, user_ref, loss_ref, out_ref, buf, sems
):
    negs = slot_ref.shape[0]
    steps = near_ref.shape[0]
    rows = out_ref.shape[0]
    scale = D ** (-0.5)
    both = near_ref[...] + far_ref[...]
    negative = both[:, :negs] * scale
    positive = jnp.sum(both[:, negs:], axis=1, keepdims=True) * scale
    usable = usable_ref[...]
    row_max = jnp.maximum(positive, jnp.max(negative, axis=1, keepdims=True))
    exp_total = jnp.exp(positive - row_max) + jnp.sum(jnp.exp(negative - row_max), axis=1, keepdims=True)
    log_total = row_max + jnp.log(exp_total)
    loss = jnp.sum(jnp.where(usable > 0, log_total - positive, 0.0)) / shard_pairs
    loss_ref[...] = jnp.full(loss_ref.shape, loss, f32)
    usable_f = usable / pairs
    pos_grad = usable_f * (jnp.exp(positive - log_total) - 1.0)
    neg_grad = (usable_f * jnp.exp(negative - log_total)).astype(bf16)
    neg_pick = (slot_ref[...] == lax.broadcasted_iota(jnp.int32, (negs, rows), 1)).astype(f32).astype(bf16)
    pos_pick = next_ref[...] == lax.broadcasted_iota(jnp.int32, (steps, rows), 1)
    grad = (dot(neg_grad, neg_pick) + jnp.where(pos_pick, pos_grad, 0.0)).astype(bf16)
    grad = jnp.transpose(grad)
    copies = []
    block = rows // 2
    for n, first in enumerate(range(0, rows, block)):
        buf[first : first + block] = (dot(grad[first : first + block], user_ref[...]) * scale).astype(bf16)
        copies.append(
            pltpu.make_async_copy(buf.at[pl.ds(first, block)], out_ref.at[pl.ds(first, block)], sems.at[n])
        )
        copies[-1].start()
    for copy in copies:
        copy.wait()


def segment_of(lengths, seq_steps):
    user_ends = jnp.cumsum(lengths)
    position = jnp.arange(seq_steps, dtype=jnp.int32)
    return jnp.sum((position[:, None] >= user_ends[None, :]).astype(jnp.int32), axis=1)


def exchange(x):
    return lax.ppermute(x, "tp", [(0, 1), (1, 0)])


def spread(x, axis):
    copies = jnp.broadcast_to(x[None], (lax.axis_size(axis),) + x.shape)
    return lax.all_to_all(copies, axis, 0, 0, tiled=True)


def ring(shards, shift):
    return [(i, (i + shift) % shards) for i in range(shards)]


def body(item_states, w_gate, w_up, w_down, w_qkv, w_out, hist_ids, hist_lengths, neg_ids):
    row_count = item_states.shape[0]
    users, shards = lax.axis_size("user"), lax.axis_size("item")
    half = D // 2
    tp = lax.axis_index("tp").astype(jnp.int32).reshape(1)
    hist_row, neg_row = hist_ids[0], neg_ids[0]
    seq_steps, negs = hist_row.shape[0], neg_row.shape[0]

    right = functools.partial(lax.ppermute, axis_name="item", perm=ring(shards, 1))
    left = functools.partial(lax.ppermute, axis_name="item", perm=ring(shards, -1))
    pieces = [w_out, right(w_out), left(w_out)]

    named = jnp.concatenate([hist_row, neg_row])
    coded = jnp.stack([named // row_count, named % row_count]).reshape(-1, LANE)
    coded = jnp.pad(coded, ((0, -coded.shape[0] % 16), (0, 0))).astype(bf16)
    mine = spread(jnp.concatenate([item_states, coded], axis=0), "user")
    mine, *pieces[-2:] = lax.optimization_barrier((mine, *pieces[-2:]))
    pieces += [right(pieces[-2]), left(pieces[-1])]
    other = exchange(mine)
    all_ids = mine[:, row_count:].reshape(users, -1)[:, : 2 * (seq_steps + negs)].astype(f32)
    all_ids = all_ids.reshape(users, 2, seq_steps + negs)

    units = w_gate.shape[1]
    gate_near, up_near = call(
        ffn_near_kernel,
        (jax.ShapeDtypeStruct((units, row_count), f32),) * 2,
        [SMEM] + [VMEM] * 3,
        (tp, mine, w_gate.T, w_up.T),
        flops=2 * row_count * units * D,
        moved=4 * units * D,
    )
    hidden, send = call(
        ffn_kernel,
        (
            jax.ShapeDtypeStruct((row_count, units), bf16),
            jax.ShapeDtypeStruct((users, row_count, LANE), bf16),
        ),
        [SMEM] + [VMEM] * 6,
        (tp, other, gate_near, up_near, w_gate.T, w_up.T, w_down),
        flops=3 * row_count * units * D,
        moved=6 * units * D,
    )
    got = exchange(send)
    partial = call(
        down_kernel,
        jax.ShapeDtypeStruct((users, row_count, LANE), bf16),
        [SMEM] + [VMEM] * 3,
        (tp, hidden, w_down, got),
        flops=row_count * units * D,
        moved=units * D,
    )
    partials = lax.all_to_all(partial, "user", 0, 0, tiled=True)
    partials, *pieces[-2:] = lax.optimization_barrier((partials, *pieces[-2:]))
    pieces += [right(pieces[-2]), left(pieces[-1])]
    emb = jnp.sum(partials.astype(f32), axis=0).astype(bf16)

    all_emb = spread(emb, "item")
    picked = pick(all_ids[:, :, :seq_steps], all_emb)
    picked, neg_ids_all = lax.optimization_barrier((picked, all_ids[:, :, seq_steps:]))
    picked_negatives = pick(neg_ids_all, all_emb)
    tokens = lax.all_to_all(picked, "user", 0, 0, tiled=True)
    segment = segment_of(hist_lengths[0], seq_steps)
    position = jnp.arange(seq_steps, dtype=jnp.int32)
    allowed = (segment[:, None] == segment[None, :]) & (position[:, None] >= position[None, :])
    allowed = allowed.astype(f32)
    usable = jnp.concatenate([segment[:-1] == segment[1:], jnp.zeros((1,), jnp.bool_)]).astype(f32)[:, None]
    item_base = lax.axis_index("item").astype(jnp.int32) * row_count
    next_slot = (jnp.concatenate([hist_row[1:], hist_row[:1]]) - item_base)[:, None]
    neg_slot = (neg_row - item_base)[:, None]
    rows = w_out.shape[0] // 2
    ends = [pieces[-2][:rows], pieces[-1][rows:]]
    masks = (allowed, usable, next_slot, neg_slot)
    tokens, picked_negatives, ends, masks = lax.optimization_barrier((tokens, picked_negatives, ends, masks))
    allowed, usable, next_slot, neg_slot = masks
    far = [right(ends[0]), left(ends[1])]
    other_tokens = exchange(tokens)

    qkv = w_qkv.transpose(1, 0, 2)
    qkv_width = qkv.shape[0] * qkv.shape[2]
    part = call(
        project_kernel,
        jax.ShapeDtypeStruct((seq_steps, qkv_width), f32),
        [SMEM] + [VMEM] * 2,
        (tp, tokens, qkv),
        flops=seq_steps * D * qkv_width,
        moved=D * qkv_width,
    )
    attended = call(
        attend_kernel,
        jax.ShapeDtypeStruct((seq_steps, HD), bf16),
        [SMEM] + [VMEM] * 4,
        (1 - tp, other_tokens, qkv, part, allowed),
        flops=seq_steps * D * qkv_width,
        moved=D * qkv_width,
    )
    attended, picked_negatives = lax.optimization_barrier((attended, picked_negatives))
    negatives = lax.all_to_all(picked_negatives, "user", 0, 0, tiled=True)
    shifts = [0, 1, -1, 2, -2, 3, -3, 4]
    heads = [attended] + [lax.ppermute(attended, "item", ring(shards, k)) for k in shifts[1:]]
    w_send, w_keep = call(
        functools.partial(fetch_kernel, shards),
        (jax.ShapeDtypeStruct((shards * w_out.shape[0], half), bf16),) * 2,
        [SMEM] + [ANY] * (shards + 1),
        [tp] + pieces + far,
        scratch=[DMAS((2 * shards + 2,))],
        moved=4 * shards * w_out.shape[0] * D,
    )

    def mixed(w, kind):
        return call(
            functools.partial(mix_kernel, shards),
            jax.ShapeDtypeStruct((seq_steps, half), kind),
            [VMEM] * (shards + 1),
            heads + [w],
            flops=seq_steps * half * D // 2,
            moved=half * D // 2,
        )

    got_user = exchange(mixed(w_send, bf16))
    own_user = mixed(w_keep, f32)
    own_user, got_user = lax.optimization_barrier((own_user, got_user))
    user_half, near = call(
        user_kernel,
        (
            jax.ShapeDtypeStruct((seq_steps, half), bf16),
            jax.ShapeDtypeStruct((seq_steps, negs + LANE), f32),
        ),
        [VMEM] * 4,
        (own_user, got_user, tokens, negatives),
        flops=seq_steps * negs * D,
        moved=negs * D,
    )
    near_other = exchange(near)
    near_other, sent_half = lax.optimization_barrier((near_other, user_half))
    other_half = exchange(sent_half)
    shard_pairs = seq_steps - hist_lengths.shape[1]
    loss, item_part = call(
        functools.partial(grad_kernel, float(users * shard_pairs), float(shard_pairs)),
        (
            jax.ShapeDtypeStruct((8, LANE), f32),
            jax.ShapeDtypeStruct((row_count, half), bf16),
        ),
        [VMEM] * 6,
        (near, near_other, usable, next_slot, neg_slot, user_half),
        scratch=[pltpu.VMEM((row_count, half), bf16), DMAS((2,))],
        out_specs=(VMEM, HBM),
        flops=2 * seq_steps * row_count * half,
        moved=row_count * half * 2,
    )
    parts = lax.all_to_all(item_part.reshape(users, row_count // users, half), "user", 0, 0, tiled=True)
    low = jnp.where(tp[0] == 0, user_half, other_half)
    high = jnp.where(tp[0] == 0, other_half, user_half)
    user_out = jnp.concatenate([low, high], axis=1)[None]
    parts, user_out = lax.optimization_barrier((parts, user_out))
    item_grad = jnp.sum(parts.astype(f32), axis=0)
    return (loss[0, :1], user_out, item_grad)


def solution(mesh):
    placed = (
        P("item", ("user", "tp")),
        P(None, ("user", "tp")),
        P(None, ("user", "tp")),
        P(("user", "tp"), None),
        P(None, None, ("item", "tp")),
        P(("item", "tp"), None),
        P("user", None),
        P("user", None),
        P("user", None),
    )
    return jax.shard_map(
        body,
        mesh=mesh,
        in_specs=placed,
        out_specs=(P("user"), P("user", None, None), P(("item", "user"), "tp")),
        check_vma=False,
    )
```
